512 devices in a mesh: narrow: 4 (over z_hi, core), wide: 128 (over x, y, z_lo).
Axes of the slice: x: 4, y: 8, z: 8 (z_hi: 2, z_lo: 4; z = z_hi * 4 + z_lo), core: 2. Of those that a mesh axis runs over, the one named last changes fastest.
Arguments:
- picture_vectors: float32 [65536, 1152], P(('narrow', 'wide')), may hold values from -1.5 to 1.5
- caption_vectors: float32 [65536, 1152], P(('narrow', 'wide')), may hold values from -1.5 to 1.5
- sharpness_factor: float32 [1], replicated, may hold values from 8 to 16
- score_shift_term: float32 [1], replicated, may hold values from -6 to -3
Outputs:
- row_loss: float32 [65536], P(('narrow', 'wide'))
- grad_images: float32 [65536, 1152], P(('narrow', 'wide'))
- grad_texts: float32 [65536, 1152], P(('narrow', 'wide'))
The draws below stay inside these ranges and needn't reach their ends.
All inputs are finite; a program needn't handle non-finite values.
Results may differ from the reference program's by a relative error of at most 0.013.
Values may be sent and summed in bfloat16 or wider, within the bound.
No kernel may reach another device: no remote copies, remote signals or barrier semaphores. Data moves between devices by JAX's collectives and lax.ppermute only.
A program may use at most 64 MiB of HBM per device.

```python
import math
import jax
import jax.numpy as jnp
from jax import lax

D = 1152
PAIRS = 128
RADIUS = 4
BATCH = 65536
N_NARROW = 4
N_WIDE = 128


def shared_rows(key):
    shared_key = jax.random.fold_in(key, 5)
    common_part = jax.random.normal(shared_key, (BATCH, D), jnp.float32)
    return common_part


def scale_field(key):
    row_key, column_key = jax.random.split(key)
    row_scale = jnp.exp(jax.random.uniform(row_key, (BATCH, 1), jnp.float32, math.log(0.3), math.log(3.0)))
    column_scale = jnp.exp(jax.random.uniform(column_key, (1, D), jnp.float32, math.log(0.3), math.log(3.0)))
    return row_scale * column_scale / math.sqrt(D)


def draw_picture_vectors(key, part):
    common_part = shared_rows(key)
    key = jax.random.fold_in(key, 11)
    values = common_part
    return jnp.clip(values * scale_field(key), -1.5, 1.5)


def draw_caption_vectors(key, part):
    common_part = shared_rows(key)
    key = jax.random.fold_in(key, 12)
    private_key, scale_key = jax.random.split(key)
    private = jax.random.normal(private_key, (BATCH, D), jnp.float32)
    values = 0.6 * common_part + 0.8 * private
    return jnp.clip(values * scale_field(scale_key), -1.5, 1.5)


def setup_inputs(seed: int = 0) -> dict:
    key_list = jax.random.split(jax.random.key(seed), 5)
    picture_vectors = draw_picture_vectors(jax.random.fold_in(key_list[4], 71), 0)
    caption_vectors = draw_caption_vectors(jax.random.fold_in(key_list[4], 71), 0)
    sharpness_factor = jnp.clip(jax.random.uniform(key_list[2], (1,), jnp.float32, 8.0, 16.0), 8.0, 16.0)
    score_shift_term = jnp.clip(jax.random.uniform(key_list[3], (1,), jnp.float32, -6.0, -3.0), -6.0, -3.0)
    return dict(picture_vectors=picture_vectors, caption_vectors=caption_vectors, sharpness_factor=sharpness_factor, score_shift_term=score_shift_term)


def unit_normalize(raw_rows):
    row_size = jnp.sqrt(lax.optimization_barrier(jnp.sum(raw_rows * raw_rows, axis=1, keepdims=True)) + 1e-06)
    return (raw_rows / row_size, row_size)

def backward(gradient, unit_rows, row_size):
    projected = lax.optimization_barrier(jnp.sum(gradient * unit_rows, axis=1, keepdims=True))
    return (gradient - projected * unit_rows) / row_size

def block_sweep_step(collected_embedding_rows, neighbor_device_rows, score_scaling_factor, window_displacement, matched_pair_score):
    similarity_matrix = lax.dot_general(collected_embedding_rows, neighbor_device_rows, (((1,), (1,)), ((), ())), preferred_element_type=jnp.float32)
    pairwise_score_matrix = score_scaling_factor * similarity_matrix + window_displacement
    target_sign = 2.0 * matched_pair_score - 1.0
    losses = jax.nn.softplus(-target_sign * pairwise_score_matrix)
    pair_label_factors = (score_scaling_factor * (jax.nn.sigmoid(pairwise_score_matrix) - matched_pair_score)).astype(jnp.bfloat16)
    picture_slice = jnp.dot(pair_label_factors, neighbor_device_rows, preferred_element_type=jnp.float32)
    caption_slice = lax.dot_general(pair_label_factors, collected_embedding_rows, (((0,), (0,)), ((), ())), preferred_element_type=jnp.float32)
    return (picture_slice, lax.optimization_barrier(jnp.sum(losses, axis=1)), caption_slice)

def reference(picture_vectors, caption_vectors, sharpness_factor, score_shift_term):
    img_unit, img_size = unit_normalize(picture_vectors)
    txt_unit, txt_size = unit_normalize(caption_vectors)
    img_low = img_unit.astype(jnp.bfloat16).reshape(N_NARROW, N_WIDE, PAIRS, D)
    caption_lower_slice = txt_unit.astype(jnp.bfloat16).reshape(N_NARROW, N_WIDE, PAIRS, D)
    score_scaling_factor = sharpness_factor[0]
    window_displacement = score_shift_term[0]
    tall_count = N_NARROW * PAIRS
    positives = (lax.broadcasted_iota(jnp.int32, (tall_count, tall_count), 0) == lax.broadcasted_iota(jnp.int32, (tall_count, tall_count), 1)).astype(jnp.float32)

    def visit(text_totals, wide_index):
        collected_embedding_rows = lax.dynamic_index_in_dim(img_low, wide_index, 1, keepdims=False).reshape(tall_count, D)
        img_grad = jnp.zeros((tall_count, D), jnp.float32)
        row_total = jnp.zeros((tall_count,), jnp.float32)
        for distance in range(-RADIUS, RADIUS + 1):
            partner_index = ((wide_index - distance) % N_WIDE).astype(jnp.int32)
            neighbor_device_rows = lax.dynamic_index_in_dim(caption_lower_slice, partner_index, 1, keepdims=False).reshape(tall_count, D)
            matched_pair_score = positives if distance == 0 else jnp.zeros((tall_count, tall_count), jnp.float32)
            picture_slice, objective_slice, caption_slice = block_sweep_step(collected_embedding_rows, neighbor_device_rows, score_scaling_factor, window_displacement, matched_pair_score)
            img_grad = img_grad + picture_slice
            row_total = row_total + objective_slice
            current = lax.dynamic_index_in_dim(text_totals, partner_index, 1, keepdims=False)
            text_totals = lax.dynamic_update_index_in_dim(text_totals, current + caption_slice.reshape(N_NARROW, PAIRS, D), partner_index, 1)
        return (text_totals, (img_grad, row_total))
    start = jnp.zeros((N_NARROW, N_WIDE, PAIRS, D), jnp.float32)
    text_totals, (img_grads, row_totals) = lax.scan(visit, start, jnp.arange(N_WIDE, dtype=jnp.int32))
    img_grads = img_grads.reshape(N_WIDE, N_NARROW, PAIRS, D).transpose(1, 0, 2, 3).reshape(BATCH, D)
    row_loss = row_totals.reshape(N_WIDE, N_NARROW, PAIRS).transpose(1, 0, 2).reshape(BATCH)
    grad_images = backward(img_grads, img_unit, img_size)
    grad_texts = backward(text_totals.reshape(BATCH, D), txt_unit, txt_size)
    return (row_loss, grad_images, grad_texts)
```

```python
import jax
import jax.numpy as jnp
from jax import lax
from jax.sharding import PartitionSpec as P

AXES = ("narrow", "wide")
SEG = 4


def unit_normalize(raw_rows):
    row_size = jnp.sqrt(jnp.sum(raw_rows * raw_rows, axis=1, keepdims=True) + 1e-06)
    return (raw_rows / row_size, row_size)


def backward(gradient, unit_rows, row_size):
    projected = jnp.sum(gradient * unit_rows, axis=1, keepdims=True)
    return (gradient - projected * unit_rows) / row_size


def routes(n_narrow, n_wide):
    chips = n_narrow // 2

    def flat(hi, core, block):
        return (hi * 2 + core) * n_wide + block % n_wide

    pairs = {name: [] for name in ("core", "hi", "a", "b", "c", "d", "e")}
    for hi in range(chips):
        for core in range(2):
            for block in range(n_wide):
                me = flat(hi, core, block)
                place = block % SEG
                rank, step = (place, 1) if core == 0 else (SEG - 1 - place, -1)
                along = [flat(hi, core, block + step * k) for k in range(SEG - rank)]
                across = flat(hi, 1 - core, block - step * SEG)
                pairs["core"].append((me, flat(hi, 1 - core, block)))
                pairs["hi"].append((me, flat(chips - 1 - hi, core, block)))
                pairs["a"].append((me, along[1] if rank <= 2 else across))
                if rank <= 2:
                    pairs["b"].append((me, along[2] if rank <= 1 else across))
                pairs["c"].append((me, along[3] if rank == 0 else across))
                pairs["d"].append((me, across))
                if rank == 3:
                    pairs["e"].append((me, across))
    return pairs


def scores(images, texts, scale, shift, labels):
    similarity = lax.dot_general(
        images, texts, (((1,), (1,)), ((), ())), preferred_element_type=jnp.float32
    )
    logits = scale * similarity + shift
    if labels is None:
        losses = jax.nn.softplus(logits)
        coef = scale * jax.nn.sigmoid(logits)
    else:
        losses = jax.nn.softplus((1.0 - 2.0 * labels) * logits)
        coef = scale * (jax.nn.sigmoid(logits) - labels)
    coef = coef.astype(jnp.bfloat16)
    text_part = lax.dot_general(
        coef, images, (((0,), (0,)), ((), ())), preferred_element_type=jnp.float32
    )
    return coef, jnp.sum(losses, axis=1, keepdims=True), text_part


def make_body(pairs):
    def send(x, name):
        return lax.ppermute(x, AXES, pairs[name])

    def send_back(x, name):
        return lax.ppermute(x, AXES, [(b, a) for a, b in pairs[name]])

    def body(picture_vectors, caption_vectors, sharpness_factor, score_shift_term):
        bf16, f32 = jnp.bfloat16, jnp.float32
        rows = picture_vectors.shape[0]
        width = picture_vectors.shape[1]
        scale, shift = sharpness_factor[0], score_shift_term[0]
        place = lax.axis_index("wide") % SEG
        rank = jnp.where(lax.axis_index("narrow") % 2 == 0, place, SEG - 1 - place)

        img_unit, img_size = unit_normalize(picture_vectors)
        txt_unit, txt_size = unit_normalize(caption_vectors)
        img_low, txt_low = img_unit.astype(bf16), txt_unit.astype(bf16)

        from_hi = send(img_low, "hi")
        from_core = send(jnp.concatenate([txt_low, img_low]), "core")
        own = jnp.concatenate([txt_low, from_core[:rows]])
        got_a = send(own, "a")
        got_b = send(own, "b")
        from_both = send(from_hi, "core")
        images = jnp.concatenate([img_low, from_core[rows:], from_hi, from_both])
        got_c = send(jnp.where(rank <= 1, own, got_a), "c")
        got_d = send(jnp.where(rank == 0, own, jnp.where(rank == 1, got_a, got_b)), "d")
        got_e = send(got_c, "e")
        got_x = jnp.where(rank == 0, got_e, got_b)

        labels = (
            lax.broadcasted_iota(jnp.int32, (4 * rows, rows), 0)
            == lax.broadcasted_iota(jnp.int32, (4 * rows, rows), 1)
        ).astype(f32)
        coef_h, loss_h, text_h = scores(images, txt_low, scale, shift, labels)
        coef_a, loss_a, text_a = scores(images, got_a, scale, shift, None)
        coef_c, loss_c, text_c = scores(images, got_c, scale, shift, None)
        coef_d, loss_d, text_d = scores(images, got_d, scale, shift, None)
        coef_x, loss_x, text_x = scores(images, got_x, scale, shift, None)

        text_c = text_c + send_back(text_x.astype(bf16), "e").astype(f32)
        back_d = send_back(text_d.astype(bf16), "d").astype(f32)
        back_c = send_back(text_c.astype(bf16), "c").astype(f32)
        text_b = text_x + jnp.where(rank >= 2, back_d, 0.0)
        back_b = send_back(text_b.astype(bf16), "b").astype(f32)
        text_a = text_a + jnp.where(rank >= 2, back_c, 0.0) + jnp.where(rank == 1, back_d, 0.0)
        back_a = send_back(text_a.astype(bf16), "a").astype(f32)
        total = (
            back_a
            + back_b
            + jnp.where(rank <= 1, back_c, 0.0)
            + jnp.where(rank == 0, back_d, 0.0)
        )
        back_core = send(total[rows:].astype(bf16), "core").astype(f32)
        txt_total = text_h + total[:rows] + back_core

        coef = jnp.concatenate([coef_h, coef_a, coef_c, coef_d, coef_x], axis=1)
        texts = jnp.concatenate([txt_low, got_a, got_c, got_d, got_x])
        img_part = jnp.dot(coef, texts, preferred_element_type=f32)
        loss = loss_h + loss_a + loss_c + loss_d + loss_x

        def packed(grad, loss):
            high = loss.astype(bf16)
            low = (loss - high.astype(f32)).astype(bf16)
            pad = jnp.zeros((grad.shape[0], 126), bf16)
            return jnp.concatenate([grad.astype(bf16), high, low, pad], axis=1)

        def unpacked(x):
            x = x.astype(f32)
            return x[:, :width], x[:, width : width + 1] + x[:, width + 1 : width + 2]

        def block(x, k):
            return x[k * rows : (k + 1) * rows]

        pick = lambda x, i, j: jnp.concatenate([block(x, i), block(x, j)])
        grad_in, loss_in = unpacked(
            send(packed(pick(img_part, 1, 3), pick(loss, 1, 3)), "core")
        )
        img_half = pick(img_part, 0, 2) + grad_in
        loss_half = pick(loss, 0, 2) + loss_in
        grad_in, loss_in = unpacked(
            send(packed(img_half[rows:], loss_half[rows:]), "hi")
        )
        img_total = img_half[:rows] + grad_in
        row_loss = (loss_half[:rows] + loss_in)[:, 0]

        grad_images = backward(img_total, img_unit, img_size)
        grad_texts = backward(txt_total, txt_unit, txt_size)
        return (row_loss, grad_images, grad_texts)

    return body


def solution(mesh):
    pairs = routes(mesh.shape["narrow"], mesh.shape["wide"])
    return jax.shard_map(
        make_body(pairs),
        mesh=mesh,
        in_specs=(P(AXES, None), P(AXES, None), P(), P()),
        out_specs=(P(AXES), P(AXES, None), P(AXES, None)),
        check_vma=False,
    )
```

```python
import jax
import jax.numpy as jnp
from jax import lax
from jax.sharding import PartitionSpec as P

AXES = ("narrow", "wide")
RUN = 4


def unit_normalize(raw_rows):
    row_size = jnp.sqrt(jnp.sum(raw_rows * raw_rows, axis=1, keepdims=True) + 1e-06)
    return (raw_rows / row_size, row_size)


def backward(gradient, unit_rows, row_size):
    projected = jnp.sum(gradient * unit_rows, axis=1, keepdims=True)
    return (gradient - projected * unit_rows) / row_size


def routes(n_wide):
    def flat(half, core, block):
        return (half * 2 + core) * n_wide + block % n_wide

    names = ("core", "pair", "text0", "text1", "text2", "text3", "small", "big")
    pairs = {name: [] for name in names}
    for half in range(2):
        for core in range(2):
            for block in range(n_wide):
                me = flat(half, core, block)
                run, pair, odd = block // RUN, block // 2 % 2, block % 2
                pairs["core"].append((me, flat(half, 1 - core, block)))
                pairs["pair"].append((me, flat(half, core, block ^ 1)))
                for j in range(4):
                    to_pair = pair if j < 2 else 1 - pair
                    to = flat(odd ^ (j & 1), half, RUN * run + 2 * to_pair + core)
                    pairs[f"text{j}"].append((me, to))
                away = RUN if pair == 0 else -RUN
                pairs["big"].append((me, flat(half, core, block + away)))
                pairs["small"].append((me, flat(half, core, block - away)))
    return pairs


def scores(images, texts, scale, shift, labels=None, mask=None):
    similarity = lax.dot_general(
        images, texts, (((1,), (1,)), ((), ())), preferred_element_type=jnp.float32
    )
    logits = scale * similarity + shift
    if labels is None:
        losses = jax.nn.softplus(logits)
        coef = scale * jax.nn.sigmoid(logits)
    else:
        losses = jax.nn.softplus((1.0 - 2.0 * labels) * logits)
        coef = scale * (jax.nn.sigmoid(logits) - labels)
    if mask is not None:
        losses = jnp.where(mask, losses, 0.0)
        coef = jnp.where(mask, coef, 0.0)
    coef = coef.astype(jnp.bfloat16)
    text_part = lax.dot_general(
        coef, images, (((0,), (0,)), ((), ())), preferred_element_type=jnp.float32
    )
    return coef, jnp.sum(losses, axis=1, keepdims=True), text_part


def make_body(pairs):
    def send(x, name):
        return lax.ppermute(x, AXES, pairs[name])

    def send_back(x, name):
        return lax.ppermute(x, AXES, [(b, a) for a, b in pairs[name]])

    def body(picture_vectors, caption_vectors, sharpness_factor, score_shift_term):
        bf16, f32 = jnp.bfloat16, jnp.float32
        rows, width = picture_vectors.shape
        scale, shift = sharpness_factor[0], score_shift_term[0]
        narrow, wide = lax.axis_index("narrow"), lax.axis_index("wide")
        half, core = narrow // 2, narrow % 2
        pair, odd = wide // 2 % 2, wide % 2

        img_unit, img_size = unit_normalize(picture_vectors)
        txt_unit, txt_size = unit_normalize(caption_vectors)
        img_low, txt_low = img_unit.astype(bf16), txt_unit.astype(bf16)

        got = [send(txt_low, f"text{j}") for j in range(4)]
        img_core = send(img_low, "core")
        img_pair = send(img_low, "pair")
        img_both = send(img_pair, "core")
        images = jnp.concatenate([img_low, img_core, img_pair, img_both])
        near = jnp.concatenate(got[:2])
        far = jnp.concatenate(got[2:])
        got_small = send(near, "small")
        got_big = send(near, "big")
        got_far = send(far, "big")

        row = lax.broadcasted_iota(jnp.int32, (4 * rows, 2 * rows), 0)
        col = lax.broadcasted_iota(jnp.int32, (4 * rows, 2 * rows), 1)
        slot, inner = col // rows, col % rows
        first = jnp.where(odd == core, 0, 3 * rows)
        second = jnp.where(odd == core, 2 * rows, rows)
        match = inner + jnp.where(slot == 0, first, second)
        labels = ((row == match) & (half == core)).astype(f32)
        img_odd = jnp.where(row < 2 * rows, odd, 1 - odd)
        txt_odd = slot ^ half
        later = jnp.where(pair == 0, txt_odd >= img_odd, txt_odd <= img_odd)
        earlier = jnp.where(pair == 0, txt_odd <= img_odd, txt_odd >= img_odd)

        coef_n, loss_n, text_n = scores(images, near, scale, shift, labels=labels)
        coef_s, loss_s, text_s = scores(images, got_small, scale, shift, mask=earlier)
        coef_b, loss_b, text_b = scores(images, got_big, scale, shift, mask=later)
        coef_f, loss_f, text_f = scores(images, far, scale, shift)
        coef_g, loss_g, text_g = scores(images, got_far, scale, shift)

        text_n = (
            text_n
            + send_back(text_s.astype(bf16), "small").astype(f32)
            + send_back(text_b.astype(bf16), "big").astype(f32)
        )
        back0 = send_back(text_n[:rows].astype(bf16), "text0")
        back1 = send_back(text_n[rows:].astype(bf16), "text1")
        text_f = text_f + send_back(text_g.astype(bf16), "big").astype(f32)
        back2 = send_back(text_f[:rows].astype(bf16), "text2")
        back3 = send_back(text_f[rows:].astype(bf16), "text3")
        txt_total = (
            back0.astype(f32) + back1.astype(f32) + back2.astype(f32) + back3.astype(f32)
        )

        coef = jnp.concatenate([coef_n, coef_s, coef_b, coef_f, coef_g], axis=1)
        texts = jnp.concatenate([near, got_small, got_big, far, got_far])
        img_part = jnp.dot(coef, texts, preferred_element_type=f32)
        loss = loss_n + loss_s + loss_b + loss_f + loss_g

        def packed(grad, loss):
            high = loss.astype(bf16)
            low = (loss - high.astype(f32)).astype(bf16)
            pad = jnp.zeros((grad.shape[0], 126), bf16)
            return jnp.concatenate([grad.astype(bf16), high, low, pad], axis=1)

        def unpacked(x):
            x = x.astype(f32)
            return x[:, :width], x[:, width : width + 1] + x[:, width + 1 : width + 2]

        def pick(x, i, j):
            return jnp.concatenate([x[k * rows : (k + 1) * rows] for k in (i, j)])

        grad_in, loss_in = unpacked(
            send(packed(pick(img_part, 1, 3), pick(loss, 1, 3)), "core")
        )
        img_half = pick(img_part, 0, 2) + grad_in
        loss_half = pick(loss, 0, 2) + loss_in
        grad_in, loss_in = unpacked(
            send(packed(img_half[rows:], loss_half[rows:]), "pair")
        )
        img_total = img_half[:rows] + grad_in
        row_loss = (loss_half[:rows] + loss_in)[:, 0]

        grad_images = backward(img_total, img_unit, img_size)
        grad_texts = backward(txt_total, txt_unit, txt_size)
        return (row_loss, grad_images, grad_texts)

    return body


def solution(mesh):
    pairs = routes(mesh.shape["wide"])
    return jax.shard_map(
        make_body(pairs),
        mesh=mesh,
        in_specs=(P(AXES, None), P(AXES, None), P(), P()),
        out_specs=(P(AXES), P(AXES, None), P(AXES, None)),
        check_vma=False,
    )
```

```python
import functools

import jax
import jax.numpy as jnp
from jax import lax
from jax.experimental import pallas as pl
from jax.experimental.pallas import tpu as pltpu
from jax.sharding import PartitionSpec as P

AXES = ("narrow", "wide")
RUN = 4
TAIL = 16


def routes(n_wide):
    def flat(half, core, block):
        return (half * 2 + core) * n_wide + block % n_wide

    def along(half, core, block, step):
        place = (half * RUN + block % RUN + step) % (2 * RUN)
        return flat(place // RUN, core, block - block % RUN + place % RUN)

    pairs = {name: [] for name in ("core", "pair", "across", "up", "down", "small", "big")}
    for half in range(2):
        for core in range(2):
            for block in range(n_wide):
                me = flat(half, core, block)
                away = RUN if block // 2 % 2 == 0 else -RUN
                pairs["core"].append((me, flat(half, 1 - core, block)))
                pairs["pair"].append((me, flat(half, core, block ^ 1)))
                pairs["across"].append((me, flat(1 - half, core, block)))
                pairs["up"].append((me, along(half, core, block, 2)))
                pairs["down"].append((me, along(half, core, block, -2)))
                pairs["big"].append((me, flat(half, core, block + away)))
                pairs["small"].append((me, flat(half, core, block - away)))
    return pairs


def call(kernel, outs, *args, after=()):
    specs = [pl.BlockSpec(memory_space=pl.ANY) for _ in after] + [
        pl.BlockSpec(memory_space=pltpu.SMEM if a.size == 1 else pltpu.VMEM) for a in args
    ]
    return pl.pallas_call(
        lambda *refs: kernel(*refs[len(after) :]),
        out_shape=outs,
        in_specs=specs,
        out_specs=jax.tree.map(lambda _: pl.BlockSpec(memory_space=pltpu.VMEM), outs),
        compiler_params=pltpu.CompilerParams(vmem_limit_bytes=8 << 20),
        cost_estimate=pl.CostEstimate(flops=1000, bytes_accessed=1000, transcendentals=0),
    )(*after, *args)


def shape(rows, width, dtype):
    return jax.ShapeDtypeStruct((rows, width), dtype)


def normalize_kernel(raw_ref, low_ref):
    raw = raw_ref[...]
    size = jnp.sqrt(jnp.sum(raw * raw, axis=1, keepdims=True) + 1e-06)
    low_ref[...] = (raw / size).astype(low_ref.dtype)


def unit_kernel(kind, rows, flag_ref, scale_ref, shift_ref, texts_ref, *refs):
    images_refs, (coef_ref, loss_ref, part_ref) = refs[:-3], refs[-3:]
    images = jnp.concatenate([r[...] for r in images_refs])
    scale, shift = scale_ref[0], shift_ref[0]
    logits = scale * lax.dot_general(
        texts_ref[...], images, (((1,), (1,)), ((), ())), preferred_element_type=jnp.float32
    ) + shift
    small = jnp.exp(-jnp.abs(logits))
    loss = jnp.maximum(logits, 0.0) + jnp.log1p(small)
    prob = jnp.where(logits >= 0.0, 1.0, small) / (1.0 + small)
    row = lax.broadcasted_iota(jnp.int32, logits.shape, 0)
    col = lax.broadcasted_iota(jnp.int32, logits.shape, 1)
    if kind == "labels":
        same = (row == col) & (row < rows)
        loss = jnp.where(same, jnp.maximum(-logits, 0.0) + jnp.log1p(small), loss)
        prob = prob - jnp.where(same, 1.0, 0.0)
    coef = scale * prob
    if kind == "mask":
        out = (col >= 2 * rows) & (flag_ref[0] != 0)
        loss = jnp.where(out, 0.0, loss)
        coef = jnp.where(out, 0.0, coef)
    coef = coef.astype(jnp.bfloat16)
    coef_ref[...] = coef
    loss_ref[...] = jnp.sum(loss, axis=0, keepdims=True)
    part_ref[...] = jnp.dot(coef, images, preferred_element_type=jnp.float32).astype(
        part_ref.dtype
    )


def image_blocks(n, rows, blocks, refs):
    coefs, texts, losses = refs[:n], refs[n : 2 * n], refs[2 * n : 3 * n]
    grads = []
    for k in blocks:
        total = None
        for coef, text in zip(coefs, texts):
            part = lax.dot_general(
                coef[:, k * rows : (k + 1) * rows],
                text[...],
                (((0,), (0,)), ((), ())),
                preferred_element_type=jnp.float32,
            )
            total = part if total is None else total + part
        grads.append(total)
    loss = losses[0][...]
    for other in losses[1:]:
        loss = loss + other[...]
    loss = jnp.concatenate([loss[:, k * rows : (k + 1) * rows] for k in blocks], axis=1)
    return grads, loss


def pack(ref, grads, loss):
    rows, width = grads[0].shape
    for k, grad in enumerate(grads):
        ref[k * rows : (k + 1) * rows, :] = grad.astype(ref.dtype)
    n = loss.shape[1]
    high = loss.astype(ref.dtype).astype(jnp.float32)
    line = jnp.concatenate([high, loss - high, jnp.zeros((1, width - 2 * n), jnp.float32)], axis=1)
    ref[len(grads) * rows :, :] = jnp.broadcast_to(line, (TAIL, width)).astype(ref.dtype)


def unpack_loss(ref, n):
    line = ref[ref.shape[0] - TAIL :, :].astype(jnp.float32)[:1]
    return line[:, :n] + line[:, n : 2 * n]


def send_kernel(n, rows, *refs):
    grads, loss = image_blocks(n, rows, (1, 3), refs)
    pack(refs[-1], grads, loss)


def keep_kernel(n, rows, *refs):
    grads, loss = image_blocks(n, rows, (0, 2), refs)
    refs[-2][:rows, :] = grads[0]
    refs[-2][rows:, :] = grads[1]
    refs[-1][...] = loss


def half_kernel(rows, grad_ref, loss_ref, got_ref, send_ref, grad_out, loss_out):
    loss = loss_ref[...] + unpack_loss(got_ref, 2 * rows)
    pack(
        send_ref,
        [grad_ref[rows:, :] + got_ref[rows : 2 * rows, :].astype(jnp.float32)],
        loss[:, rows:],
    )
    grad_out[...] = grad_ref[:rows, :] + got_ref[:rows, :].astype(jnp.float32)
    loss_out[...] = loss[:, :rows]


def project(raw, grad):
    size = jnp.sqrt(jnp.sum(raw * raw, axis=1, keepdims=True) + 1e-06)
    unit = raw / size
    along = jnp.sum(grad * unit, axis=1, keepdims=True)
    return (grad - along * unit) / size


def image_end_kernel(rows, raw_ref, grad_ref, loss_ref, got_ref, grad_out, loss_out):
    loss_out[...] = loss_ref[...] + unpack_loss(got_ref, rows)
    grad = grad_ref[...] + got_ref[:rows, :].astype(jnp.float32)
    grad_out[...] = project(raw_ref[...], grad)


def text_end_kernel(raw_ref, *refs):
    grad = refs[0][...].astype(jnp.float32)
    for other in refs[1:-1]:
        grad = grad + other[...].astype(jnp.float32)
    refs[-1][...] = project(raw_ref[...], grad)


def sum_kernel(*refs):
    upper, lower = refs[-2:]
    rows = upper.shape[0]
    total = refs[0][...].astype(jnp.float32)
    for other in refs[1:-2]:
        total = total + other[...].astype(jnp.float32)
    upper[...] = total[:rows].astype(upper.dtype)
    lower[...] = total[rows:].astype(lower.dtype)


def make_body(pairs):
    def send(x, name):
        return lax.ppermute(x, AXES, pairs[name])

    def send_back(x, name):
        return lax.ppermute(x, AXES, [(b, a) for a, b in pairs[name]])

    def body(picture_vectors, caption_vectors, sharpness_factor, score_shift_term):
        bf16, f32, i32 = jnp.bfloat16, jnp.float32, jnp.int32
        rows, width = picture_vectors.shape
        wide = lax.axis_index("wide")
        pair, odd = wide // 2 % 2, wide % 2

        nothing = jnp.zeros((1,), i32)
        out_big = (odd == pair).astype(i32).reshape(1)
        out_small = (odd != pair).astype(i32).reshape(1)

        txt_low = call(normalize_kernel, shape(rows, width, bf16), caption_vectors)
        img_low = call(normalize_kernel, shape(rows, width, bf16), picture_vectors)

        near = jnp.concatenate([txt_low, send(txt_low, "across")])
        far = jnp.concatenate([send(txt_low, "up"), send(txt_low, "down")])
        img_own = jnp.concatenate([img_low, send(img_low, "pair")])
        img_core = send(img_own, "core")
        got_small = send(near, "small")
        got_big = send(near, "big")
        got_far = send(far, "big")

        def unit(kind, flag, texts, dtype):
            outs = (
                shape(2 * rows, 4 * rows, bf16),
                shape(1, 4 * rows, f32),
                shape(2 * rows, width, dtype),
            )
            kernel = functools.partial(unit_kernel, kind, rows)
            images = [
                img_own[:rows], img_core[:rows], img_own[rows:], img_core[rows:]
            ]
            return call(kernel, outs, flag, sharpness_factor, score_shift_term, texts, *images)

        coef_n, loss_n, text_n = unit("labels", nothing, near, f32)
        coef_s, loss_s, text_s = unit("mask", out_small, got_small, bf16)
        coef_b, loss_b, text_b = unit("mask", out_big, got_big, bf16)
        coef_f, loss_f, text_f = unit("plain", nothing, far, f32)
        coef_g, loss_g, text_g = unit("plain", nothing, got_far, bf16)

        ordered = lax.optimization_barrier
        back_b, back_s = send_back(text_b, "big"), send_back(text_s, "small")
        total = ordered(text_n + back_b.astype(f32))
        total = ordered(total + back_s.astype(f32))
        total = ordered(jnp.concatenate([total[rows:], total[:rows]]))
        away, home = ordered((total[:rows].astype(bf16), total[rows:]))
        back_across = send_back(away, "across")
        total = text_f + send_back(text_g, "big").astype(f32)
        far0, far1 = ordered((total[:rows].astype(bf16), total[rows:].astype(bf16)))
        back_up, back_down = send_back(far0, "up"), send_back(far1, "down")

        units = (
            coef_n, coef_s, coef_b, coef_f, coef_g,
            near, got_small, got_big, far, got_far,
            loss_n, loss_s, loss_b, loss_f, loss_g,
        )
        packed = call(
            functools.partial(send_kernel, 5, rows), shape(2 * rows + TAIL, width, bf16), *units
        )
        img_part, loss = call(
            functools.partial(keep_kernel, 5, rows),
            (shape(2 * rows, width, f32), shape(1, 2 * rows, f32)),
            *units,
        )
        packed, img_part, loss = call(
            functools.partial(half_kernel, rows),
            (shape(rows + TAIL, width, bf16), shape(rows, width, f32), shape(1, rows, f32)),
            img_part, loss, send(packed, "core"),
        )
        grad_images, row_loss = call(
            functools.partial(image_end_kernel, rows),
            (shape(rows, width, f32), shape(1, rows, f32)),
            picture_vectors, img_part, loss, send(packed, "pair"),
        )
        grad_texts = call(
            text_end_kernel, shape(rows, width, f32),
            caption_vectors, home, back_across, back_up, back_down,
        )
        return (row_loss.reshape(rows), grad_images, grad_texts)

    return body


def solution(mesh):
    pairs = routes(mesh.shape["wide"])
    return jax.shard_map(
        make_body(pairs),
        mesh=mesh,
        in_specs=(P(AXES, None), P(AXES, None), P(), P()),
        out_specs=(P(AXES), P(AXES, None), P(AXES, None)),
        check_vma=False,
    )
```

```python
import functools

import jax
import jax.numpy as jnp
from jax import lax
from jax.experimental import pallas as pl
from jax.experimental.pallas import tpu as pltpu
from jax.sharding import PartitionSpec as P

AXES = ("narrow", "wide")
RUN = 4
TAIL = 16


def routes(n_wide):
    def flat(half, core, block):
        return (half * 2 + core) * n_wide + block % n_wide

    def along(half, core, block, step):
        place = (half * RUN + block % RUN + step) % (2 * RUN)
        return flat(place // RUN, core, block - block % RUN + place % RUN)

    pairs = {name: [] for name in ("core", "pair", "across", "up", "down", "small", "big")}
    for half in range(2):
        for core in range(2):
            for block in range(n_wide):
                me = flat(half, core, block)
                away = RUN if block // 2 % 2 == 0 else -RUN
                pairs["core"].append((me, flat(half, 1 - core, block)))
                pairs["pair"].append((me, flat(half, core, block ^ 1)))
                pairs["across"].append((me, flat(1 - half, core, block)))
                pairs["up"].append((me, along(half, core, block, 2)))
                pairs["down"].append((me, along(half, core, block, -2)))
                pairs["big"].append((me, flat(half, core, block + away)))
                pairs["small"].append((me, flat(half, core, block - away)))
    return pairs


def call(kernel, outs, *args, after=()):
    specs = [pl.BlockSpec(memory_space=pl.ANY) for _ in after] + [
        pl.BlockSpec(memory_space=pltpu.SMEM if a.size == 1 else pltpu.VMEM) for a in args
    ]
    return pl.pallas_call(
        lambda *refs: kernel(*refs[len(after) :]),
        out_shape=outs,
        in_specs=specs,
        out_specs=jax.tree.map(lambda _: pl.BlockSpec(memory_space=pltpu.VMEM), outs),
        compiler_params=pltpu.CompilerParams(vmem_limit_bytes=8 << 20),
        cost_estimate=pl.CostEstimate(flops=1000, bytes_accessed=1000, transcendentals=0),
    )(*after, *args)


def shape(rows, width, dtype):
    return jax.ShapeDtypeStruct((rows, width), dtype)


def normalize_kernel(raw_ref, low_ref):
    raw = raw_ref[...]
    size = jnp.sqrt(jnp.sum(raw * raw, axis=1, keepdims=True) + 1e-06)
    low_ref[...] = (raw / size).astype(low_ref.dtype)


def unit_kernel(kind, rows, flag_ref, scale_ref, shift_ref, texts_ref, *refs):
    images_refs, (coef_ref, loss_ref, part_ref) = refs[:-3], refs[-3:]
    images = jnp.concatenate([r[...] for r in images_refs])
    scale, shift = scale_ref[0], shift_ref[0]
    logits = scale * lax.dot_general(
        texts_ref[...], images, (((1,), (1,)), ((), ())), preferred_element_type=jnp.float32
    ) + shift
    small = jnp.exp(-jnp.abs(logits))
    loss = jnp.maximum(logits, 0.0) + jnp.log1p(small)
    prob = jnp.where(logits >= 0.0, 1.0, small) / (1.0 + small)
    row = lax.broadcasted_iota(jnp.int32, logits.shape, 0)
    col = lax.broadcasted_iota(jnp.int32, logits.shape, 1)
    if kind == "labels":
        same = (row == col) & (row < rows)
        loss = jnp.where(same, jnp.maximum(-logits, 0.0) + jnp.log1p(small), loss)
        prob = prob - jnp.where(same, 1.0, 0.0)
    coef = scale * prob
    if kind == "mask":
        out = (col >= 2 * rows) & (flag_ref[0] != 0)
        loss = jnp.where(out, 0.0, loss)
        coef = jnp.where(out, 0.0, coef)
    coef = coef.astype(jnp.bfloat16)
    coef_ref[...] = coef
    loss_ref[...] = jnp.sum(loss, axis=0, keepdims=True)
    part_ref[...] = jnp.dot(coef, images, preferred_element_type=jnp.float32).astype(
        part_ref.dtype
    )


def image_blocks(n, rows, blocks, refs):
    coefs, texts, losses = refs[:n], refs[n : 2 * n], refs[2 * n : 3 * n]
    grads = []
    for k in blocks:
        total = None
        for coef, text in zip(coefs, texts):
            part = lax.dot_general(
                coef[:, k * rows : (k + 1) * rows],
                text[...],
                (((0,), (0,)), ((), ())),
                preferred_element_type=jnp.float32,
            )
            total = part if total is None else total + part
        grads.append(total)
    loss = losses[0][...]
    for other in losses[1:]:
        loss = loss + other[...]
    loss = jnp.concatenate([loss[:, k * rows : (k + 1) * rows] for k in blocks], axis=1)
    return grads, loss


def pack(ref, grads, loss):
    rows, width = grads[0].shape
    for k, grad in enumerate(grads):
        ref[k * rows : (k + 1) * rows, :] = grad.astype(ref.dtype)
    n = loss.shape[1]
    high = loss.astype(ref.dtype).astype(jnp.float32)
    line = jnp.concatenate([high, loss - high, jnp.zeros((1, width - 2 * n), jnp.float32)], axis=1)
    ref[len(grads) * rows :, :] = jnp.broadcast_to(line, (TAIL, width)).astype(ref.dtype)


def unpack_loss(ref, n):
    line = ref[ref.shape[0] - TAIL :, :].astype(jnp.float32)[:1]
    return line[:, :n] + line[:, n : 2 * n]


def send_kernel(n, rows, *refs):
    grads, loss = image_blocks(n, rows, (2, 3), refs)
    pack(refs[-1], grads, loss)


def keep_kernel(n, rows, *refs):
    grads, loss = image_blocks(n, rows, (0, 1), refs)
    refs[-2][:rows, :] = grads[0]
    refs[-2][rows:, :] = grads[1]
    refs[-1][...] = loss


def half_kernel(rows, grad_ref, loss_ref, got_ref, send_ref, grad_out, loss_out):
    loss = loss_ref[...] + unpack_loss(got_ref, 2 * rows)
    pack(
        send_ref,
        [grad_ref[rows:, :] + got_ref[rows : 2 * rows, :].astype(jnp.float32)],
        loss[:, rows:],
    )
    grad_out[...] = grad_ref[:rows, :] + got_ref[:rows, :].astype(jnp.float32)
    loss_out[...] = loss[:, :rows]


def project(raw, grad):
    size = jnp.sqrt(jnp.sum(raw * raw, axis=1, keepdims=True) + 1e-06)
    unit = raw / size
    along = jnp.sum(grad * unit, axis=1, keepdims=True)
    return (grad - along * unit) / size


def image_end_kernel(rows, raw_ref, grad_ref, loss_ref, got_ref, grad_out, loss_out):
    loss_out[...] = loss_ref[...] + unpack_loss(got_ref, rows)
    grad = grad_ref[...] + got_ref[:rows, :].astype(jnp.float32)
    grad_out[...] = project(raw_ref[...], grad)


def text_end_kernel(raw_ref, *refs):
    grad = refs[0][...].astype(jnp.float32)
    for other in refs[1:-1]:
        grad = grad + other[...].astype(jnp.float32)
    refs[-1][...] = project(raw_ref[...], grad)


def sum_kernel(*refs):
    upper, lower = refs[-2:]
    rows = upper.shape[0]
    total = refs[0][...].astype(jnp.float32)
    for other in refs[1:-2]:
        total = total + other[...].astype(jnp.float32)
    upper[...] = total[:rows].astype(upper.dtype)
    lower[...] = total[rows:].astype(lower.dtype)


def make_body(pairs):
    def send(x, name):
        return lax.ppermute(x, AXES, pairs[name])

    def send_back(x, name):
        return lax.ppermute(x, AXES, [(b, a) for a, b in pairs[name]])

    def body(picture_vectors, caption_vectors, sharpness_factor, score_shift_term):
        bf16, f32, i32 = jnp.bfloat16, jnp.float32, jnp.int32
        rows, width = picture_vectors.shape
        wide = lax.axis_index("wide")
        pair, odd = wide // 2 % 2, wide % 2

        nothing = jnp.zeros((1,), i32)
        out_big = (odd == pair).astype(i32).reshape(1)
        out_small = (odd != pair).astype(i32).reshape(1)

        txt_low = call(normalize_kernel, shape(rows, width, bf16), caption_vectors)
        img_low = call(normalize_kernel, shape(rows, width, bf16), picture_vectors)

        near = jnp.concatenate([txt_low, send(txt_low, "across")])
        far = jnp.concatenate([send(txt_low, "up"), send(txt_low, "down")])
        img_own = jnp.concatenate([img_low, send(img_low, "pair")])
        img_core = send(img_own, "core")
        got_small = send(near, "small")
        got_big = send(near, "big")
        got_far = send(far, "big")

        def unit(kind, flag, texts, dtype):
            outs = (
                shape(2 * rows, 4 * rows, bf16),
                shape(1, 4 * rows, f32),
                shape(2 * rows, width, dtype),
            )
            kernel = functools.partial(unit_kernel, kind, rows)
            images = [
                img_own[:rows], img_core[:rows], img_own[rows:], img_core[rows:]
            ]
            return call(kernel, outs, flag, sharpness_factor, score_shift_term, texts, *images)

        coef_n, loss_n, text_n = unit("labels", nothing, near, f32)
        coef_s, loss_s, text_s = unit("mask", out_small, got_small, bf16)
        coef_b, loss_b, text_b = unit("mask", out_big, got_big, bf16)
        coef_f, loss_f, text_f = unit("plain", nothing, far, f32)
        coef_g, loss_g, text_g = unit("plain", nothing, got_far, bf16)

        ordered = lax.optimization_barrier
        back_b, back_s = send_back(text_b, "big"), send_back(text_s, "small")
        total = ordered(text_n + back_b.astype(f32))
        total = ordered(total + back_s.astype(f32))
        total = ordered(jnp.concatenate([total[rows:], total[:rows]]))
        away, home = ordered((total[:rows].astype(bf16), total[rows:]))
        back_across = send_back(away, "across")
        total = text_f + send_back(text_g, "big").astype(f32)
        far0, far1 = ordered((total[:rows].astype(bf16), total[rows:].astype(bf16)))
        back_up, back_down = send_back(far0, "up"), send_back(far1, "down")

        units = (
            coef_n, coef_s, coef_b, coef_f, coef_g,
            near, got_small, got_big, far, got_far,
            loss_n, loss_s, loss_b, loss_f, loss_g,
        )
        packed = call(
            functools.partial(send_kernel, 5, rows), shape(2 * rows + TAIL, width, bf16), *units
        )
        img_part, loss = call(
            functools.partial(keep_kernel, 5, rows),
            (shape(2 * rows, width, f32), shape(1, 2 * rows, f32)),
            *units,
        )
        packed, img_part, loss = call(
            functools.partial(half_kernel, rows),
            (shape(rows + TAIL, width, bf16), shape(rows, width, f32), shape(1, rows, f32)),
            img_part, loss, send(packed, "pair"),
        )
        grad_images, row_loss = call(
            functools.partial(image_end_kernel, rows),
            (shape(rows, width, f32), shape(1, rows, f32)),
            picture_vectors, img_part, loss, send(packed, "core"),
        )
        total = ordered(home + back_across.astype(f32))
        total = ordered(total + back_up.astype(f32) + back_down.astype(f32))
        grad_texts = call(
            text_end_kernel, shape(rows, width, f32), caption_vectors, total
        )
        return (row_loss.reshape(rows), grad_images, grad_texts)

    return body


def solution(mesh):
    pairs = routes(mesh.shape["wide"])
    return jax.shard_map(
        make_body(pairs),
        mesh=mesh,
        in_specs=(P(AXES, None), P(AXES, None), P(), P()),
        out_specs=(P(AXES), P(AXES, None), P(AXES, None)),
        check_vma=False,
    )
```

```python
import functools

import jax
import jax.numpy as jnp
from jax import lax
from jax.experimental import pallas as pl
from jax.experimental.pallas import tpu as pltpu
from jax.sharding import PartitionSpec as P

AXES = ("narrow", "wide")
RUN = 4
TAIL = 16


def routes(n_wide):
    def flat(half, core, block):
        return (half * 2 + core) * n_wide + block % n_wide

    def along(half, core, block, step):
        place = (half * RUN + block % RUN + step) % (2 * RUN)
        return flat(place // RUN, core, block - block % RUN + place % RUN)

    pairs = {name: [] for name in ("core", "pair", "across", "up", "down", "small", "big")}
    for half in range(2):
        for core in range(2):
            for block in range(n_wide):
                me = flat(half, core, block)
                away = RUN if block // 2 % 2 == 0 else -RUN
                pairs["core"].append((me, flat(half, 1 - core, block)))
                pairs["pair"].append((me, flat(half, core, block ^ 1)))
                pairs["across"].append((me, flat(1 - half, core, block)))
                pairs["up"].append((me, along(half, core, block, 2)))
                pairs["down"].append((me, along(half, core, block, -2)))
                pairs["big"].append((me, flat(half, core, block + away)))
                pairs["small"].append((me, flat(half, core, block - away)))
    return pairs


def call(kernel, outs, *args, after=()):
    specs = [pl.BlockSpec(memory_space=pl.ANY) for _ in after] + [
        pl.BlockSpec(memory_space=pltpu.SMEM if a.size == 1 else pltpu.VMEM) for a in args
    ]
    return pl.pallas_call(
        lambda *refs: kernel(*refs[len(after) :]),
        out_shape=outs,
        in_specs=specs,
        out_specs=jax.tree.map(lambda _: pl.BlockSpec(memory_space=pltpu.VMEM), outs),
        compiler_params=pltpu.CompilerParams(vmem_limit_bytes=8 << 20),
        cost_estimate=pl.CostEstimate(flops=1000, bytes_accessed=1000, transcendentals=0),
    )(*after, *args)


def shape(rows, width, dtype):
    return jax.ShapeDtypeStruct((rows, width), dtype)


def normalize_kernel(raw_ref, low_ref):
    raw = raw_ref[...]
    size = jnp.sqrt(jnp.sum(raw * raw, axis=1, keepdims=True) + 1e-06)
    low_ref[...] = (raw / size).astype(low_ref.dtype)


def unit_kernel(kind, rows, flag_ref, scale_ref, shift_ref, texts_ref, *refs):
    images_refs, (coef_ref, loss_ref, part_ref) = refs[:-3], refs[-3:]
    images = jnp.concatenate([r[...] for r in images_refs])
    scale, shift = scale_ref[0], shift_ref[0]
    logits = scale * lax.dot_general(
        texts_ref[...], images, (((1,), (1,)), ((), ())), preferred_element_type=jnp.float32
    ) + shift
    small = jnp.exp(-jnp.abs(logits))
    loss = jnp.maximum(logits, 0.0) + jnp.log1p(small)
    prob = jnp.where(logits >= 0.0, 1.0, small) / (1.0 + small)
    row = lax.broadcasted_iota(jnp.int32, logits.shape, 0)
    col = lax.broadcasted_iota(jnp.int32, logits.shape, 1)
    if kind == "labels":
        same = (row == col) & (row < rows)
        loss = jnp.where(same, jnp.maximum(-logits, 0.0) + jnp.log1p(small), loss)
        prob = prob - jnp.where(same, 1.0, 0.0)
    coef = scale * prob
    if kind == "mask":
        out = (col >= 2 * rows) & (flag_ref[0] != 0)
        loss = jnp.where(out, 0.0, loss)
        coef = jnp.where(out, 0.0, coef)
    coef = coef.astype(jnp.bfloat16)
    coef_ref[...] = coef
    loss_ref[...] = jnp.sum(loss, axis=0, keepdims=True)
    part_ref[...] = jnp.dot(coef, images, preferred_element_type=jnp.float32).astype(
        part_ref.dtype
    )


def image_blocks(n, rows, blocks, refs):
    coefs, texts, losses = refs[:n], refs[n : 2 * n], refs[2 * n : 3 * n]
    grads = []
    for k in blocks:
        total = None
        for coef, text in zip(coefs, texts):
            part = lax.dot_general(
                coef[:, k * rows : (k + 1) * rows],
                text[...],
                (((0,), (0,)), ((), ())),
                preferred_element_type=jnp.float32,
            )
            total = part if total is None else total + part
        grads.append(total)
    loss = losses[0][...]
    for other in losses[1:]:
        loss = loss + other[...]
    loss = jnp.concatenate([loss[:, k * rows : (k + 1) * rows] for k in blocks], axis=1)
    return grads, loss


def pack(ref, grads, loss):
    rows, width = grads[0].shape
    for k, grad in enumerate(grads):
        ref[k * rows : (k + 1) * rows, :] = grad.astype(ref.dtype)
    n = loss.shape[1]
    high = loss.astype(ref.dtype).astype(jnp.float32)
    line = jnp.concatenate([high, loss - high, jnp.zeros((1, width - 2 * n), jnp.float32)], axis=1)
    ref[len(grads) * rows :, :] = jnp.broadcast_to(line, (TAIL, width)).astype(ref.dtype)


def unpack_loss(ref, n):
    line = ref[ref.shape[0] - TAIL :, :].astype(jnp.float32)[:1]
    return line[:, :n] + line[:, n : 2 * n]


def send_kernel(n, rows, *refs):
    grads, loss = image_blocks(n, rows, (2, 3), refs)
    pack(refs[-1], grads, loss)


def keep_kernel(n, rows, *refs):
    grads, loss = image_blocks(n, rows, (0, 1), refs)
    refs[-2][:rows, :] = grads[0]
    refs[-2][rows:, :] = grads[1]
    refs[-1][...] = loss


def half_kernel(rows, grad_ref, loss_ref, got_ref, send_ref, grad_out, loss_out):
    loss = loss_ref[...] + unpack_loss(got_ref, 2 * rows)
    pack(
        send_ref,
        [grad_ref[rows:, :] + got_ref[rows : 2 * rows, :].astype(jnp.float32)],
        loss[:, rows:],
    )
    grad_out[...] = grad_ref[:rows, :] + got_ref[:rows, :].astype(jnp.float32)
    loss_out[...] = loss[:, :rows]


def project(raw, grad):
    size = jnp.sqrt(jnp.sum(raw * raw, axis=1, keepdims=True) + 1e-06)
    unit = raw / size
    along = jnp.sum(grad * unit, axis=1, keepdims=True)
    return (grad - along * unit) / size


def end_kernel(
    rows, images_ref, grad_ref, loss_ref, got_ref, texts_ref, total_ref, img_out, loss_out, txt_out
):
    loss_out[...] = loss_ref[...] + unpack_loss(got_ref, rows)
    grad = grad_ref[...] + got_ref[:rows, :].astype(jnp.float32)
    img_out[...] = project(images_ref[...], grad)
    txt_out[...] = project(texts_ref[...], total_ref[...])


def sum_kernel(*refs):
    upper, lower = refs[-2:]
    rows = upper.shape[0]
    total = refs[0][...].astype(jnp.float32)
    for other in refs[1:-2]:
        total = total + other[...].astype(jnp.float32)
    upper[...] = total[:rows].astype(upper.dtype)
    lower[...] = total[rows:].astype(lower.dtype)


def make_body(pairs):
    def send(x, name):
        return lax.ppermute(x, AXES, pairs[name])

    def send_back(x, name):
        return lax.ppermute(x, AXES, [(b, a) for a, b in pairs[name]])

    def body(picture_vectors, caption_vectors, sharpness_factor, score_shift_term):
        bf16, f32, i32 = jnp.bfloat16, jnp.float32, jnp.int32
        rows, width = picture_vectors.shape
        wide = lax.axis_index("wide")
        pair, odd = wide // 2 % 2, wide % 2

        nothing = jnp.zeros((1,), i32)
        out_big = (odd == pair).astype(i32).reshape(1)
        out_small = (odd != pair).astype(i32).reshape(1)

        txt_low = call(normalize_kernel, shape(rows, width, bf16), caption_vectors)
        img_low = call(normalize_kernel, shape(rows, width, bf16), picture_vectors)

        near = jnp.concatenate([txt_low, send(txt_low, "across")])
        far = jnp.concatenate([send(txt_low, "up"), send(txt_low, "down")])
        img_own = jnp.concatenate([img_low, send(img_low, "pair")])
        img_core = send(img_own, "core")
        got_small = send(near, "small")
        got_big = send(near, "big")
        got_far = send(far, "big")

        def unit(kind, flag, texts, dtype):
            outs = (
                shape(2 * rows, 4 * rows, bf16),
                shape(1, 4 * rows, f32),
                shape(2 * rows, width, dtype),
            )
            kernel = functools.partial(unit_kernel, kind, rows)
            images = [
                img_own[:rows], img_core[:rows], img_own[rows:], img_core[rows:]
            ]
            return call(kernel, outs, flag, sharpness_factor, score_shift_term, texts, *images)

        coef_n, loss_n, text_n = unit("labels", nothing, near, f32)
        coef_s, loss_s, text_s = unit("mask", out_small, got_small, bf16)
        coef_b, loss_b, text_b = unit("mask", out_big, got_big, bf16)
        coef_f, loss_f, text_f = unit("plain", nothing, far, f32)
        coef_g, loss_g, text_g = unit("plain", nothing, got_far, bf16)

        ordered = lax.optimization_barrier
        back_b, back_s = send_back(text_b, "big"), send_back(text_s, "small")
        total = ordered(text_n + back_b.astype(f32))
        total = ordered(total + back_s.astype(f32))
        total = ordered(jnp.concatenate([total[rows:], total[:rows]]))
        away, home = ordered((total[:rows].astype(bf16), total[rows:]))
        back_across = send_back(away, "across")
        total = text_f + send_back(text_g, "big").astype(f32)
        far0, far1 = ordered((total[:rows].astype(bf16), total[rows:].astype(bf16)))
        back_up, back_down = send_back(far0, "up"), send_back(far1, "down")

        units = (
            coef_n, coef_s, coef_b, coef_f, coef_g,
            near, got_small, got_big, far, got_far,
            loss_n, loss_s, loss_b, loss_f, loss_g,
        )
        packed = call(
            functools.partial(send_kernel, 5, rows), shape(2 * rows + TAIL, width, bf16), *units
        )
        img_part, loss = call(
            functools.partial(keep_kernel, 5, rows),
            (shape(2 * rows, width, f32), shape(1, 2 * rows, f32)),
            *units,
        )
        packed, img_part, loss = call(
            functools.partial(half_kernel, rows),
            (shape(rows + TAIL, width, bf16), shape(rows, width, f32), shape(1, rows, f32)),
            img_part, loss, send(packed, "pair"),
        )
        total = ordered(home + back_across.astype(f32))
        total = ordered(total + back_up.astype(f32) + back_down.astype(f32))
        grad_images, row_loss, grad_texts = call(
            functools.partial(end_kernel, rows),
            (shape(rows, width, f32), shape(1, rows, f32), shape(rows, width, f32)),
            picture_vectors, img_part, loss, send(packed, "core"), caption_vectors, total,
        )
        return (row_loss.reshape(rows), grad_images, grad_texts)

    return body


def solution(mesh):
    pairs = routes(mesh.shape["wide"])
    return jax.shard_map(
        make_body(pairs),
        mesh=mesh,
        in_specs=(P(AXES, None), P(AXES, None), P(), P()),
        out_specs=(P(AXES), P(AXES, None), P(AXES, None)),
        check_vma=False,
    )
```
